32 devices in a mesh: section: 4 (over y, x), dp: 8 (over z, core).
Axes of the slice: x: 2, y: 2, z: 4, core: 2. Of those that a mesh axis runs over, the one named last changes fastest.
Arguments:
- enc_in: bfloat16 [4, 2, 4096, 1152], P('section', None, 'dp'), may hold values from -6 to 6
- dec_in: bfloat16 [4, 2, 4096, 1152], P('section', None, 'dp'), may hold values from -6 to 6
- cotangent: bfloat16 [4, 2, 4096, 1152], P('section', None, 'dp'), may hold values from -0.23925781 to 0.23925781
- w_proj: float32 [4, 1152, 1152], P('section', 'dp'), may hold values from -0.1875 to 0.1875
- w_skip: float32 [4, 2304, 1152], P('section', 'dp'), may hold values from -0.125 to 0.125
- m_proj: float32 [4, 1152, 1152], P('section', 'dp'), may hold values from -3 to 3
- v_proj: float32 [4, 1152, 1152], P('section', 'dp'), may hold values from 0.05 to 1
- m_skip: float32 [4, 2304, 1152], P('section', 'dp'), may hold values from -3 to 3
- v_skip: float32 [4, 2304, 1152], P('section', 'dp'), may hold values from 0.05 to 1
Outputs:
- dec_out: bfloat16 [4, 2, 4096, 1152], P('section', None, 'dp')
- enc_grad: bfloat16 [4, 2, 4096, 1152], P('section', None, 'dp')
- dec_grad: bfloat16 [4, 2, 4096, 1152], P('section', None, 'dp')
- new_w_proj: float32 [4, 1152, 1152], P('section', 'dp')
- new_m_proj: float32 [4, 1152, 1152], P('section', 'dp')
- new_v_proj: float32 [4, 1152, 1152], P('section', 'dp')
- new_w_skip: float32 [4, 2304, 1152], P('section', 'dp')
- new_m_skip: float32 [4, 2304, 1152], P('section', 'dp')
- new_v_skip: float32 [4, 2304, 1152], P('section', 'dp')
The draws below stay inside these ranges and needn't reach their ends.
All inputs are finite; a program needn't handle non-finite values.
Results may differ from the reference program's by a relative error of at most 0.025.
Values may be sent and summed in bfloat16 or wider, within the bound.
No kernel may reach another device: no remote copies, remote signals or barrier semaphores. Data moves between devices by JAX's collectives and lax.ppermute only.
A program may use at most 128 MiB of HBM per device.

```python
import math
import jax
import jax.numpy as jnp
from jax import lax

D = 1152
MB = 2
TOKENS = 4096
N_SECTION = 4


def level_of(own_key, dims, cuts, least, high):
    factor_of = 1.0
    for position, parts in cuts:
        heights = jax.random.uniform(jax.random.fold_in(jax.random.fold_in(own_key, 6), position), (parts,), jnp.float32, least / len(cuts), high / len(cuts))
        factor_of = factor_of * jnp.repeat(jnp.exp(heights), dims[position] // parts).reshape((-1,) + (1,) * (len(dims) - 1 - position))
    return factor_of


def scatter_about(stream_key, dims, deviation, most, cuts=(), held_as=jnp.bfloat16):
    result = deviation * jax.random.normal(stream_key, dims, jnp.float32)
    if cuts:
        result = result * level_of(stream_key, dims, cuts, -0.22, 0.18)
    return jnp.clip(result, -most, most).astype(held_as)


def setup_inputs(seed: int = 0) -> dict:
    keys = jax.random.split(jax.random.key(seed), 10)
    return {
        "enc_in": scatter_about(keys[0], (N_SECTION, MB, TOKENS, D), 1.0, 6.0, ((0, 4), (2, 8))),
        "dec_in": scatter_about(keys[1], (N_SECTION, MB, TOKENS, D), 1.0, 6.0, ((0, 4), (2, 8))),
        "cotangent": scatter_about(keys[2], (N_SECTION, MB, TOKENS, D), 0.04, 0.23925781, ((0, 4), (2, 8))),
        "w_proj": scatter_about(keys[3], (N_SECTION, D, D), D ** -0.5, 0.1875, ((0, 4), (1, 8)), jnp.float32),
        "w_skip": scatter_about(keys[4], (N_SECTION, 2 * D, D), (2 * D) ** -0.5, 0.125, ((0, 4), (1, 8)), jnp.float32),
        "m_proj": scatter_about(keys[5], (N_SECTION, D, D), 0.5, 3.0, ((0, 4), (1, 8)), jnp.float32),
        "v_proj": jnp.clip(jnp.exp(math.log(1.0) - 2.9957323 * jax.random.uniform(keys[6], (N_SECTION, D, D), jnp.float32) ** level_of(keys[6], (N_SECTION, D, D), ((0, 4), (1, 8)), -0.2, 0.2)), 0.05, 1.0),
        "m_skip": scatter_about(keys[7], (N_SECTION, 2 * D, D), 0.5, 3.0, ((0, 4), (1, 8)), jnp.float32),
        "v_skip": jnp.clip(jnp.exp(math.log(1.0) - 2.9957323 * jax.random.uniform(keys[8], (N_SECTION, 2 * D, D), jnp.float32) ** level_of(keys[8], (N_SECTION, 2 * D, D), ((0, 4), (1, 8)), -0.2, 0.2)), 0.05, 1.0),
    }


half_root = 0.7071067811865476
gauss_norm = 0.3989422804014327
beta_one = 0.9
beta_two = 0.95
learn_rate = 0.002
adam_eps = 1e-08
correct_one = 1.0 - 0.9 ** 10
correct_two = 1.0 - 0.95 ** 10

def gelu_parts(preact):
    normal_cdf = 0.5 * (1.0 + lax.erf(preact * half_root))
    density = jnp.exp(-0.5 * preact * preact) * gauss_norm
    return (preact * normal_cdf, normal_cdf + preact * density)

def adam_update(weight, moment, second, grad):
    new_moment = beta_one * moment + (1.0 - beta_one) * grad
    new_second = beta_two * second + (1.0 - beta_two) * grad * grad
    step_size = new_moment / correct_one / (jnp.sqrt(new_second / correct_two) + adam_eps)
    return (weight - learn_rate * step_size, new_moment, new_second)

def partner_of(section):
    return (section + N_SECTION // 2) % N_SECTION

def reference(enc_in, dec_in, cotangent, w_proj, w_skip, m_proj, v_proj, m_skip, v_skip):
    rows = MB * TOKENS
    proj_half = w_proj.astype(jnp.bfloat16)
    skip_half = w_skip.astype(jnp.bfloat16)
    skips = []
    for section in range(N_SECTION):
        enc_rows = enc_in[section].reshape(rows, D)
        skips.append(jnp.dot(enc_rows, proj_half[section], preferred_element_type=jnp.float32).astype(jnp.bfloat16))
    dec_outs = []
    dec_grads = []
    grad_skips = []
    skip_grads = [None] * N_SECTION
    for section in range(N_SECTION):
        dec_rows = dec_in[section].reshape(rows, D)
        joined = jnp.concatenate([dec_rows, skips[partner_of(section)]], axis=1)
        preact = jnp.dot(joined, skip_half[section], preferred_element_type=jnp.float32)
        activated, gelu_slope = gelu_parts(preact)
        dec_outs.append(activated.astype(jnp.bfloat16).reshape(MB, TOKENS, D))
        out_grad = cotangent[section].reshape(rows, D).astype(jnp.float32)
        pre_grad = (out_grad * gelu_slope).astype(jnp.bfloat16)
        input_grad = jnp.dot(pre_grad, skip_half[section].T, preferred_element_type=jnp.float32)
        dec_grads.append(input_grad[:, :D].astype(jnp.bfloat16).reshape(MB, TOKENS, D))
        skip_grads[partner_of(section)] = input_grad[:, D:].astype(jnp.bfloat16)
        grad_skips.append(jnp.dot(joined.T, pre_grad, preferred_element_type=jnp.float32))
    enc_grads = []
    grad_projs = []
    for section in range(N_SECTION):
        enc_rows = enc_in[section].reshape(rows, D)
        enc_grads.append(jnp.dot(skip_grads[section], proj_half[section].T, preferred_element_type=jnp.float32).astype(jnp.bfloat16).reshape(MB, TOKENS, D))
        grad_projs.append(jnp.dot(enc_rows.T, skip_grads[section], preferred_element_type=jnp.float32))
    new_w_proj, new_m_proj, new_v_proj = adam_update(w_proj, m_proj, v_proj, jnp.stack(grad_projs, 0))
    new_w_skip, new_m_skip, new_v_skip = adam_update(w_skip, m_skip, v_skip, jnp.stack(grad_skips, 0))
    return (jnp.stack(dec_outs, 0), jnp.stack(enc_grads, 0), jnp.stack(dec_grads, 0), new_w_proj, new_m_proj, new_v_proj, new_w_skip, new_m_skip, new_v_skip)
```

```python
import jax
import jax.numpy as jnp
from jax import lax
from jax.sharding import PartitionSpec as P

half_root = 0.7071067811865476
gauss_norm = 0.3989422804014327
beta_one = 0.9
beta_two = 0.95
learn_rate = 0.002
adam_eps = 1e-08
correct_one = 1.0 - 0.9**10
correct_two = 1.0 - 0.95**10


def gelu_parts(preact):
    normal_cdf = 0.5 * (1.0 + lax.erf(preact * half_root))
    density = jnp.exp(-0.5 * preact * preact) * gauss_norm
    return (preact * normal_cdf, normal_cdf + preact * density)


def adam_update(weight, moment, second, grad):
    new_moment = beta_one * moment + (1.0 - beta_one) * grad
    new_second = beta_two * second + (1.0 - beta_two) * grad * grad
    step_size = new_moment / correct_one / (jnp.sqrt(new_second / correct_two) + adam_eps)
    return (weight - learn_rate * step_size, new_moment, new_second)


def to_partner(value):
    count = lax.axis_size("section")
    pairs = [(s, (s + count // 2) % count) for s in range(count)]
    return lax.ppermute(value, "section", pairs)


def chip_count():
    return lax.axis_size("dp") // 2


def to_chips(value, pairs):
    return lax.ppermute(value, "dp", [(2 * a + c, 2 * b + c) for a, b in pairs for c in range(2)])


def chip_flip(value, mask):
    return to_chips(value, [(z, z ^ mask) for z in range(chip_count())])


def core_flip(value):
    return lax.ppermute(value, "dp", [(d, d ^ 1) for d in range(lax.axis_size("dp"))])


def gather_chips(piece):
    held = [piece]
    step = chip_count() // 2
    found = {0: piece}
    while step:
        came = {k + step: chip_flip(found[k], step) for k in sorted(found)}
        found.update(came)
        step //= 2
    return [found[k] for k in range(chip_count())]


def plus(*terms):
    total = terms[0].astype(jnp.float32)
    for term in terms[1:]:
        total = total + term.astype(jnp.float32)
    return total


def scatter_chips(blocks):
    chips = chip_count()
    step = 1
    while step < chips // 2:
        came = {k: chip_flip(blocks[k + step], step) for k in range(0, chips, 2 * step) if k}
        for k in came:
            blocks[k] = plus(blocks[k], came[k]).astype(jnp.bfloat16)
        step *= 2
    terms, step = [blocks[0]], 1
    while step < chips:
        terms.append(chip_flip(blocks[step], step))
        step *= 2
    return plus(*terms)


def gather_rows(piece):
    chips = chip_count()
    place = lax.axis_index("dp")
    chip, core = place // 2, place % 2
    mine = gather_chips(piece)
    whole = jnp.zeros((chips, 2) + piece.shape, piece.dtype)
    for k in range(chips):
        whole = lax.dynamic_update_slice(whole, mine[k][None, None], (chip ^ k, core, 0, 0))
        whole = lax.dynamic_update_slice(whole, core_flip(mine[k])[None, None], (chip ^ k, 1 - core, 0, 0))
    return whole.reshape(-1, piece.shape[1])


def scatter_rows(total):
    chips = chip_count()
    place = lax.axis_index("dp")
    chip, core = place // 2, place % 2
    split = total.reshape(chips, 2, -1, total.shape[1])
    keep = lax.dynamic_index_in_dim(split, core, 1, keepdims=False)
    send = lax.dynamic_index_in_dim(split, 1 - core, 1, keepdims=False)
    both = plus(keep, core_flip(send)).astype(jnp.bfloat16)
    return scatter_chips([lax.dynamic_index_in_dim(both, chip ^ k, 0, keepdims=False) for k in range(chips)])


def matmul(left, right):
    return jnp.dot(left, right, preferred_element_type=jnp.float32)


def body(enc_in, dec_in, cotangent, w_proj, w_skip, m_proj, v_proj, m_skip, v_skip):
    micro, tokens_here, width = enc_in.shape[1:]
    rows = micro * tokens_here
    enc_rows = enc_in[0].reshape(rows, width)
    dec_rows = dec_in[0].reshape(rows, width)
    out_grad = cotangent[0].reshape(rows, width)

    proj_other = to_partner(w_proj[0].astype(jnp.bfloat16))
    enc_other = to_partner(enc_rows)
    skip_full = gather_rows(w_skip[0].astype(jnp.bfloat16))
    proj_full = gather_rows(proj_other)
    upper, lower = skip_full[:width], skip_full[width:]

    skip = matmul(enc_other, proj_full).astype(jnp.bfloat16)
    preact = matmul(dec_rows, upper) + matmul(skip, lower)
    activated, gelu_slope = gelu_parts(preact)
    dec_out = activated.astype(jnp.bfloat16)
    pre_grad = (out_grad.astype(jnp.float32) * gelu_slope).astype(jnp.bfloat16)

    skip_grad = jnp.einsum("rk,jk->rj", pre_grad, lower, preferred_element_type=jnp.float32).astype(jnp.bfloat16)
    grad_proj = jnp.einsum("rj,rk->jk", enc_other, skip_grad, preferred_element_type=jnp.float32).astype(jnp.bfloat16)
    proj_sum = to_partner(scatter_rows(grad_proj).astype(jnp.bfloat16)).astype(jnp.float32)
    enc_grad = to_partner(
        jnp.einsum("rk,jk->rj", skip_grad, proj_full, preferred_element_type=jnp.float32).astype(jnp.bfloat16)
    )
    grad_upper = jnp.einsum("rj,rk->jk", dec_rows, pre_grad, preferred_element_type=jnp.float32).astype(jnp.bfloat16)
    grad_lower = jnp.einsum("rj,rk->jk", skip, pre_grad, preferred_element_type=jnp.float32).astype(jnp.bfloat16)
    skip_sum = scatter_rows(jnp.concatenate([grad_upper, grad_lower], axis=0))
    dec_grad = jnp.einsum("rk,jk->rj", pre_grad, upper, preferred_element_type=jnp.float32).astype(jnp.bfloat16)

    new_proj = adam_update(w_proj[0], m_proj[0], v_proj[0], proj_sum)
    new_skip = adam_update(w_skip[0], m_skip[0], v_skip[0], skip_sum)
    streams = tuple(value.reshape(1, micro, tokens_here, width) for value in (dec_out, enc_grad, dec_grad))
    return streams + tuple(value[None] for value in new_proj + new_skip)


def solution(mesh):
    tokens = P("section", None, "dp", None)
    weights = P("section", "dp", None)
    return jax.shard_map(
        body,
        mesh=mesh,
        in_specs=(tokens,) * 3 + (weights,) * 6,
        out_specs=(tokens,) * 3 + (weights,) * 6,
        check_vma=False,
    )
```

```python
import math

import jax
import jax.numpy as jnp
from jax import lax
from jax.experimental import pallas as pl
from jax.experimental.pallas import tpu as pltpu
from jax.sharding import PartitionSpec as P

half_root = 0.7071067811865476
gauss_norm = 0.3989422804014327
beta_one = 0.9
beta_two = 0.95
learn_rate = 0.002
adam_eps = 1e-08
correct_one = 1.0 - 0.9**10
correct_two = 1.0 - 0.95**10


def gelu_parts(preact):
    normal_cdf = 0.5 * (1.0 + lax.erf(preact * half_root))
    density = jnp.exp(-0.5 * preact * preact) * gauss_norm
    return (preact * normal_cdf, normal_cdf + preact * density)


def adam_update(weight, moment, second, grad):
    new_moment = beta_one * moment + (1.0 - beta_one) * grad
    new_second = beta_two * second + (1.0 - beta_two) * grad * grad
    step_size = new_moment / correct_one / (jnp.sqrt(new_second / correct_two) + adam_eps)
    return (weight - learn_rate * step_size, new_moment, new_second)


def to_partner(value):
    count = lax.axis_size("section")
    pairs = [(s, (s + count // 2) % count) for s in range(count)]
    return lax.ppermute(value, "section", pairs)


def chip_count():
    return lax.axis_size("dp") // 2


def to_chips(value, pairs):
    return lax.ppermute(value, "dp", [(2 * a + c, 2 * b + c) for a, b in pairs for c in range(2)])


def chip_flip(value, mask):
    return to_chips(value, [(z, z ^ mask) for z in range(chip_count())])


def core_flip(value):
    return lax.ppermute(value, "dp", [(d, d ^ 1) for d in range(lax.axis_size("dp"))])


def gather_first(piece):
    found = {0: piece}
    step = chip_count() // 2
    while step > 1:
        found.update({k + step: chip_flip(found[k], step) for k in sorted(found)})
        step //= 2
    found[1] = chip_flip(piece, 1)
    return found


def gather_last(found):
    for k in range(2, chip_count(), 2):
        found[k + 1] = chip_flip(found[k], 1)
    return [found[k] for k in range(chip_count())]


def plus(*terms):
    total = terms[0].astype(jnp.float32)
    for term in terms[1:]:
        total = total + term.astype(jnp.float32)
    return total


def scatter_near(blocks):
    return {k: chip_flip(blocks[k + 1], 1) for k in range(2, len(blocks), 2)}


def scatter_on(blocks, came):
    held = {k: plus(blocks[k], came[k]).astype(jnp.bfloat16) for k in came}
    step = 2
    while step < len(blocks) // 2:
        for k in range(2 * step, len(blocks), 2 * step):
            held[k] = plus(held[k], chip_flip(held[k + step], step)).astype(jnp.bfloat16)
        step *= 2
    return [chip_flip(held[2**n], 2**n) for n in range(1, len(blocks).bit_length() - 1)]


def assemble(found):
    place = lax.axis_index("dp")
    chip, core = place // 2, place % 2
    rows, width = found[0].shape
    whole = jnp.zeros((chip_count(), 2, rows, width), found[0].dtype)
    for k, piece in enumerate(found):
        whole = lax.dynamic_update_slice(whole, piece[None, None], (chip ^ k, core, 0, 0))
        whole = lax.dynamic_update_slice(whole, core_flip(piece)[None, None], (chip ^ k, 1 - core, 0, 0))
    return whole.reshape(-1, width)


def interleave(parts, refs, target, sems):
    copies = []
    for (rows, start, stride), ref in zip(parts, refs):
        if rows == stride:
            copies.append(pltpu.make_async_copy(ref, target, sems.at[len(copies)]))
            continue
        for d in range(ref.shape[0] // rows):
            copies.append(
                pltpu.make_async_copy(
                    ref.at[pl.ds(d * rows, rows)], target.at[pl.ds(d * stride + start, rows)], sems.at[len(copies)]
                )
            )
    for copy in copies:
        copy.start()
    for copy in copies:
        copy.wait()


def copy_count(weights, parts):
    return sum(1 if rows == stride else w.shape[0] // rows for w, (rows, _, stride) in zip(weights, parts))


def row_call(compute, row_arrays, weights, parts, out_count, tile_rows, vmem_mib, start=0, rows=None):
    width = row_arrays[0].shape[1]
    rows = rows or row_arrays[0].shape[0]
    tile = math.gcd(math.gcd(rows, start), tile_rows)
    count = copy_count(weights, parts)

    def kernel(*refs):
        ins = refs[: len(row_arrays)]
        weight_refs = refs[len(row_arrays) : len(row_arrays) + len(weights)]
        outs = refs[len(row_arrays) + len(weights) :][:out_count]
        whole, sems = refs[-2:]

        @pl.when(pl.program_id(0) == 0)
        def _():
            interleave(parts, weight_refs, whole, sems)

        compute(ins, whole, outs)

    block = pl.BlockSpec((tile, width), lambda i: (i, 0))
    taken = pl.BlockSpec((tile, width), lambda i: (i + start // tile, 0))
    return pl.pallas_call(
        kernel,
        grid=(rows // tile,),
        in_specs=[taken] * len(row_arrays) + [pl.BlockSpec(memory_space=pl.ANY)] * len(weights),
        out_specs=[block] * out_count,
        out_shape=[jax.ShapeDtypeStruct((rows, width), jnp.bfloat16)] * out_count,
        scratch_shapes=[
            pltpu.VMEM((sum(w.shape[0] for w in weights), width), jnp.bfloat16),
            pltpu.SemaphoreType.DMA((count,)),
        ],
        compiler_params=pltpu.CompilerParams(vmem_limit_bytes=vmem_mib * 2**20),
        cost_estimate=pl.CostEstimate(flops=COST, bytes_accessed=COST, transcendentals=0),
    )(*row_arrays, *weights)


COST = 1000


def dot_nn(left, right):
    return jnp.dot(left, right, preferred_element_type=jnp.float32)


def dot_nt(left, right):
    return lax.dot_general(left, right, (((1,), (1,)), ((), ())), preferred_element_type=jnp.float32)


def dot_tn(left, right):
    return lax.dot_general(left, right, (((0,), (0,)), ((), ())), preferred_element_type=jnp.float32)


def project(parts, weight, vmem_mib):
    width = weight.shape[1]
    rows = sum(part.shape[0] for part in parts)

    def kernel(*refs):
        at = 0
        for ref, part in zip(refs, parts):
            refs[-1][at : at + part.shape[0]] = dot_nn(ref[...], refs[-2][...]).astype(jnp.bfloat16)
            at += part.shape[0]

    return pl.pallas_call(
        kernel,
        out_shape=jax.ShapeDtypeStruct((rows, width), jnp.bfloat16),
        compiler_params=pltpu.CompilerParams(vmem_limit_bytes=vmem_mib * 2**20),
        cost_estimate=pl.CostEstimate(flops=COST, bytes_accessed=COST, transcendentals=0),
    )(*parts, weight)


def project_back(ins, whole, outs):
    outs[0][...] = dot_nt(ins[0][...], whole[...]).astype(jnp.bfloat16)


def upper_back(ins, whole, outs):
    width = ins[0].shape[1]
    outs[0][...] = dot_nt(ins[0][...], whole[:width]).astype(jnp.bfloat16)


def middle(ins, whole, outs):
    dec, skip, out_grad = ins
    rows, width = dec.shape
    part = math.gcd(rows, 256)
    for at in range(0, rows, part):
        here = slice(at, at + part)
        preact = dot_nn(dec[here], whole[:width]) + dot_nn(skip[here], whole[width:])
        activated, gelu_slope = gelu_parts(preact)
        outs[0][here] = activated.astype(jnp.bfloat16)
        pre_grad = (out_grad[here].astype(jnp.float32) * gelu_slope).astype(jnp.bfloat16)
        outs[1][here] = pre_grad
        outs[2][here] = dot_nt(pre_grad, whole[width:]).astype(jnp.bfloat16)


def weight_grad(lefts, right):
    rows, width = right.shape
    tile = math.gcd(width, 384)
    steps = width // tile
    parts = [(n, part) for n, left in enumerate(lefts) for part in left]

    def kernel(*refs):
        step = pl.program_id(0)
        right_ref, out_ref = refs[-2:]
        for n in range(len(lefts)):

            @pl.when(step // steps == n)
            def _(n=n):
                total, at = 0.0, 0
                for ref, (owner, part) in zip(refs, parts):
                    if owner == n:
                        total = total + dot_tn(ref[...], right_ref[at : at + part.shape[0]])
                        at += part.shape[0]
                out_ref[...] = total.astype(jnp.bfloat16)

    def spec(n, part):
        return pl.BlockSpec((part.shape[0], tile), lambda i: (0, jnp.clip(i - n * steps, 0, steps - 1)))

    return pl.pallas_call(
        kernel,
        grid=(len(lefts) * steps,),
        in_specs=[spec(n, part) for n, part in parts]
        + [pl.BlockSpec((rows, width), lambda i: (0, 0), pipeline_mode=pl.Buffered(1))],
        out_specs=pl.BlockSpec((tile, width), lambda i: (i, 0)),
        out_shape=jax.ShapeDtypeStruct((len(lefts) * width, width), jnp.bfloat16),
        compiler_params=pltpu.CompilerParams(vmem_limit_bytes=16 * 2**20),
        cost_estimate=pl.CostEstimate(flops=COST, bytes_accessed=COST, transcendentals=0),
    )(*[part for _, part in parts], right)


def pair_split(total):
    core = lax.axis_index("dp") % 2
    split = total.reshape(chip_count(), 2, -1, total.shape[1])
    keep = lax.dynamic_index_in_dim(split, core, 1, keepdims=False)
    return keep, lax.dynamic_index_in_dim(split, 1 - core, 1, keepdims=False)


def pair_send(total):
    keep, send = pair_split(total)
    return keep, core_flip(send)


def pair_sum(keep, came):
    chip = lax.axis_index("dp") // 2
    both = plus(keep, came).astype(jnp.bfloat16)
    return [lax.dynamic_index_in_dim(both, chip ^ k, 0, keepdims=False) for k in range(chip_count())]


def body(enc_in, dec_in, cotangent, w_proj, w_skip, m_proj, v_proj, m_skip, v_skip):
    micro, tokens_here, width = enc_in.shape[1:]
    rows = micro * tokens_here
    enc_rows = enc_in[0].reshape(rows, width)
    dec_rows = dec_in[0].reshape(rows, width)
    out_grad = cotangent[0].reshape(rows, width)
    together = lax.optimization_barrier

    enc_cuts = [rows * n // 8 for n in (5, 6)]
    proj_half, skip_half = w_proj[0].astype(jnp.bfloat16), w_skip[0].astype(jnp.bfloat16)
    stride = skip_half.shape[0]
    cut = stride // 48 * 16
    proj_piece = to_partner(proj_half)
    head = gather_first(skip_half[:cut])
    proj_piece, head, tail, enc0 = together((proj_piece, head, skip_half[cut:], enc_rows[: enc_cuts[0]]))
    enc0 = to_partner(enc0)
    proj_found = gather_first(proj_piece)
    tail = gather_first(tail)
    enc0, proj_found, tail, head, enc1 = together((enc0, proj_found, tail, head, enc_rows[enc_cuts[0] : enc_cuts[1]]))
    enc1 = to_partner(enc1)
    proj_found = gather_last(proj_found)
    head = gather_last(head)
    enc1, proj_found, tail, head, enc2 = together((enc1, proj_found, tail, head, enc_rows[enc_cuts[1] :]))
    enc2 = to_partner(enc2)
    proj_whole = assemble(proj_found)
    skip_w = [assemble(head), assemble(gather_last(tail))]
    enc_other = (enc0, enc1, enc2)
    skip_parts = [(cut, 0, stride), (stride - cut, cut, stride)]

    skip = project(enc_other, proj_whole, 20)
    dec_out, pre_grad, skip_grad = row_call(
        middle, [dec_rows, skip, out_grad], skip_w, skip_parts, 3, 512, 30
    )
    cuts = [0] + [rows * n // 8 for n in (1, 3, 4, 8)]

    def back(n, value):
        return row_call(
            project_back, [value], [proj_whole], [(1, 0, 1)], 1, 256, 16, start=cuts[n], rows=cuts[n + 1] - cuts[n]
        )[0]

    grad_proj = weight_grad([enc_other], skip_grad)
    grad_proj, skip_grad = together((grad_proj, skip_grad))
    proj_keep, proj_came = pair_send(grad_proj)
    enc0 = back(0, skip_grad)
    proj_keep, proj_came, enc0, pre_grad, skip_grad = together((proj_keep, proj_came, enc0, pre_grad, skip_grad))
    enc0 = to_partner(enc0)
    proj_blocks = pair_sum(proj_keep, proj_came)
    proj_near = scatter_near(proj_blocks)
    skip_keep, skip_send = pair_split(weight_grad([(dec_rows,), (skip,)], pre_grad))
    enc1 = back(1, skip_grad)
    enc0, proj_blocks, proj_near, skip_keep, skip_send, enc1, skip_grad = together(
        (enc0, proj_blocks, proj_near, skip_keep, skip_send, enc1, skip_grad)
    )
    enc1 = to_partner(enc1)
    proj_on = scatter_on(proj_blocks, proj_near)
    proj_one = chip_flip(proj_blocks[1], 1)
    skip_came = core_flip(skip_send)
    enc2 = back(2, skip_grad)
    enc3 = back(3, skip_grad)
    enc1, proj_blocks, proj_on, proj_one, skip_keep, skip_came, enc2, enc3 = together(
        (enc1, proj_blocks, proj_on, proj_one, skip_keep, skip_came, enc2, enc3)
    )
    enc2 = to_partner(enc2)
    proj_sum = to_partner(plus(proj_blocks[0], proj_one, *proj_on).astype(jnp.bfloat16))
    skip_blocks = pair_sum(skip_keep, skip_came)
    skip_near = scatter_near(skip_blocks)
    enc2, proj_sum, skip_blocks, skip_near, enc3, pre_grad = together(
        (enc2, proj_sum, skip_blocks, skip_near, enc3, pre_grad)
    )
    proj_sum = proj_sum.astype(jnp.float32)
    enc3 = to_partner(enc3)
    skip_on = scatter_on(skip_blocks, skip_near)
    skip_one = chip_flip(skip_blocks[1], 1)
    skip_sum = plus(skip_blocks[0], skip_one, *skip_on)
    (dec_grad,) = row_call(upper_back, [pre_grad], skip_w, skip_parts, 1, 256, 20)
    enc_grad = jnp.zeros_like(enc_rows)
    for at, part in zip(cuts, (enc0, enc1, enc2, enc3)):
        enc_grad = lax.dynamic_update_slice(enc_grad, part, (at, 0))

    new_proj = adam_update(w_proj[0], m_proj[0], v_proj[0], proj_sum)
    new_skip = adam_update(w_skip[0], m_skip[0], v_skip[0], skip_sum)
    streams = tuple(value.reshape(1, micro, tokens_here, width) for value in (dec_out, enc_grad, dec_grad))
    return streams + tuple(value[None] for value in new_proj + new_skip)


def solution(mesh):
    tokens = P("section", None, "dp", None)
    weights = P("section", "dp", None)
    return jax.shard_map(
        body,
        mesh=mesh,
        in_specs=(tokens,) * 3 + (weights,) * 6,
        out_specs=(tokens,) * 3 + (weights,) * 6,
        check_vma=False,
    )
```

```python
import math

import jax
import jax.numpy as jnp
from jax import lax
from jax.experimental import pallas as pl
from jax.experimental.pallas import tpu as pltpu
from jax.sharding import PartitionSpec as P

half_root = 0.7071067811865476
gauss_norm = 0.3989422804014327
beta_one = 0.9
beta_two = 0.95
learn_rate = 0.002
adam_eps = 1e-08
correct_one = 1.0 - 0.9**10
correct_two = 1.0 - 0.95**10


def gelu_parts(preact):
    normal_cdf = 0.5 * (1.0 + lax.erf(preact * half_root))
    density = jnp.exp(-0.5 * preact * preact) * gauss_norm
    return (preact * normal_cdf, normal_cdf + preact * density)


def adam_update(weight, moment, second, grad):
    new_moment = beta_one * moment + (1.0 - beta_one) * grad
    new_second = beta_two * second + (1.0 - beta_two) * grad * grad
    step_size = new_moment / correct_one / (jnp.sqrt(new_second / correct_two) + adam_eps)
    return (weight - learn_rate * step_size, new_moment, new_second)


def to_partner(value):
    count = lax.axis_size("section")
    pairs = [(s, (s + count // 2) % count) for s in range(count)]
    return lax.ppermute(value, "section", pairs)


def chip_count():
    return lax.axis_size("dp") // 2


def to_chips(value, pairs):
    return lax.ppermute(value, "dp", [(2 * a + c, 2 * b + c) for a, b in pairs for c in range(2)])


def chip_flip(value, mask):
    return to_chips(value, [(z, z ^ mask) for z in range(chip_count())])


def core_flip(value):
    return lax.ppermute(value, "dp", [(d, d ^ 1) for d in range(lax.axis_size("dp"))])


def gather_first(piece):
    found = {0: piece}
    step = chip_count() // 2
    while step > 1:
        found.update({k + step: chip_flip(found[k], step) for k in sorted(found)})
        step //= 2
    found[1] = chip_flip(piece, 1)
    return found


def gather_last(found):
    return {k + 1: chip_flip(found[k], 1) for k in range(2, chip_count(), 2)}


def plus(*terms):
    total = terms[0].astype(jnp.float32)
    for term in terms[1:]:
        total = total + term.astype(jnp.float32)
    return total


def scatter_near(blocks):
    return {k: chip_flip(blocks[k + 1], 1) for k in range(2, len(blocks), 2)}


def scatter_on(blocks, came):
    held = {k: plus(blocks[k], came[k]).astype(jnp.bfloat16) for k in came}
    step = 2
    while step < len(blocks) // 2:
        for k in range(2 * step, len(blocks), 2 * step):
            held[k] = plus(held[k], chip_flip(held[k + step], step)).astype(jnp.bfloat16)
        step *= 2
    return [chip_flip(held[2**n], 2**n) for n in range(1, len(blocks).bit_length() - 1)]


def assemble(found, whole=None):
    place = lax.axis_index("dp")
    chip, core = place // 2, place % 2
    rows, width = found[min(found)].shape
    if whole is None:
        whole = jnp.zeros((2 * chip_count() * rows, width), found[0].dtype)
    whole = whole.reshape(chip_count(), 2, rows, width)
    for k, piece in found.items():
        whole = lax.dynamic_update_slice(whole, piece[None, None], (chip ^ k, core, 0, 0))
        whole = lax.dynamic_update_slice(whole, core_flip(piece)[None, None], (chip ^ k, 1 - core, 0, 0))
    return whole.reshape(-1, width)


def interleave(parts, refs, target, sems, half):
    copies = []
    for (rows, start, stride), ref in zip(parts, refs):
        if rows == stride:
            copies.append(pltpu.make_async_copy(ref, target, sems.at[len(copies)]))
            continue
        count = ref.shape[0] // rows
        taken = range(count) if half is None else range(half * count // 2, (half + 1) * count // 2)
        for d in taken:
            to = (d - taken[0]) * stride + start
            copies.append(
                pltpu.make_async_copy(
                    ref.at[pl.ds(d * rows, rows)], target.at[pl.ds(to, rows)], sems.at[len(copies)]
                )
            )
    for copy in copies:
        copy.start()
    for copy in copies:
        copy.wait()


def copy_count(weights, parts):
    return sum(1 if rows == stride else w.shape[0] // rows for w, (rows, _, stride) in zip(weights, parts))


def row_call(compute, row_arrays, weights, parts, out_count, tile_rows, vmem_mib, start=0, rows=None, out_type=jnp.bfloat16, half=None):
    width = row_arrays[0].shape[1]
    rows = rows or row_arrays[0].shape[0]
    tile = math.gcd(math.gcd(rows, start), tile_rows)
    count = copy_count(weights, parts)

    def kernel(*refs):
        ins = refs[: len(row_arrays)]
        weight_refs = refs[len(row_arrays) : len(row_arrays) + len(weights)]
        outs = refs[len(row_arrays) + len(weights) :][:out_count]
        whole, sems = refs[-2:]

        @pl.when(pl.program_id(0) == 0)
        def _():
            interleave(parts, weight_refs, whole, sems, half)

        compute(ins, whole, outs)

    block = pl.BlockSpec((tile, width), lambda i: (i, 0))
    taken = pl.BlockSpec((tile, width), lambda i: (i + start // tile, 0))
    return pl.pallas_call(
        kernel,
        grid=(rows // tile,),
        in_specs=[taken] * len(row_arrays) + [pl.BlockSpec(memory_space=pl.ANY)] * len(weights),
        out_specs=[block] * out_count,
        out_shape=[jax.ShapeDtypeStruct((rows, width), out_type)] * out_count,
        scratch_shapes=[
            pltpu.VMEM((sum(w.shape[0] for w in weights) // (1 if half is None else 2), width), jnp.bfloat16),
            pltpu.SemaphoreType.DMA((count,)),
        ],
        compiler_params=pltpu.CompilerParams(vmem_limit_bytes=vmem_mib * 2**20),
        cost_estimate=pl.CostEstimate(flops=COST, bytes_accessed=COST, transcendentals=0),
    )(*row_arrays, *weights)


COST = 1000


def dot_nn(left, right):
    return jnp.dot(left, right, preferred_element_type=jnp.float32)


def dot_nt(left, right):
    return lax.dot_general(left, right, (((1,), (1,)), ((), ())), preferred_element_type=jnp.float32)


def dot_tn(left, right):
    return lax.dot_general(left, right, (((0,), (0,)), ((), ())), preferred_element_type=jnp.float32)


def project(parts, weight, vmem_mib):
    width = weight.shape[1]
    rows = sum(part.shape[0] for part in parts)

    def kernel(*refs):
        at = 0
        for ref, part in zip(refs, parts):
            refs[-1][at : at + part.shape[0]] = dot_nn(ref[...], refs[-2][...]).astype(jnp.bfloat16)
            at += part.shape[0]

    return pl.pallas_call(
        kernel,
        out_shape=jax.ShapeDtypeStruct((rows, width), jnp.bfloat16),
        compiler_params=pltpu.CompilerParams(vmem_limit_bytes=vmem_mib * 2**20),
        cost_estimate=pl.CostEstimate(flops=COST, bytes_accessed=COST, transcendentals=0),
    )(*parts, weight)


def project_back(ins, whole, outs):
    outs[0][...] = dot_nt(ins[0][...], whole[...]).astype(jnp.bfloat16)


def decoder_part(ins, whole, outs):
    outs[0][...] = dot_nn(ins[0][...], whole[...])


def middle(ins, whole, outs):
    from_dec, skip, out_grad = ins
    rows, width = skip.shape
    part = math.gcd(rows, 256)
    for at in range(0, rows, part):
        here = slice(at, at + part)
        preact = from_dec[here] + dot_nn(skip[here], whole[...])
        activated, gelu_slope = gelu_parts(preact)
        outs[0][here] = activated.astype(jnp.bfloat16)
        pre_grad = (out_grad[here].astype(jnp.float32) * gelu_slope).astype(jnp.bfloat16)
        outs[1][here] = pre_grad
        outs[2][here] = dot_nt(pre_grad, whole[...]).astype(jnp.bfloat16)


def weight_grad(lefts, right):
    rows, width = right.shape
    tile = math.gcd(width, 384)
    steps = width // tile
    parts = [(n, part) for n, left in enumerate(lefts) for part in left]

    def kernel(*refs):
        step = pl.program_id(0)
        right_ref, out_ref = refs[-2:]
        for n in range(len(lefts)):

            @pl.when(step // steps == n)
            def _(n=n):
                total, at = 0.0, 0
                for ref, (owner, part) in zip(refs, parts):
                    if owner == n:
                        total = total + dot_tn(ref[...], right_ref[at : at + part.shape[0]])
                        at += part.shape[0]
                out_ref[...] = total.astype(jnp.bfloat16)

    def spec(n, part):
        return pl.BlockSpec((part.shape[0], tile), lambda i: (0, jnp.clip(i - n * steps, 0, steps - 1)))

    return pl.pallas_call(
        kernel,
        grid=(len(lefts) * steps,),
        in_specs=[spec(n, part) for n, part in parts]
        + [pl.BlockSpec((rows, width), lambda i: (0, 0), pipeline_mode=pl.Buffered(1))],
        out_specs=pl.BlockSpec((tile, width), lambda i: (i, 0)),
        out_shape=jax.ShapeDtypeStruct((len(lefts) * width, width), jnp.bfloat16),
        compiler_params=pltpu.CompilerParams(vmem_limit_bytes=16 * 2**20),
        cost_estimate=pl.CostEstimate(flops=COST, bytes_accessed=COST, transcendentals=0),
    )(*[part for _, part in parts], right)


def pair_split(total):
    core = lax.axis_index("dp") % 2
    split = total.reshape(chip_count(), 2, -1, total.shape[1])
    keep = lax.dynamic_index_in_dim(split, core, 1, keepdims=False)
    return keep, lax.dynamic_index_in_dim(split, 1 - core, 1, keepdims=False)


def pair_send(total):
    keep, send = pair_split(total)
    return keep, core_flip(send)


def pair_sum(keep, came):
    chip = lax.axis_index("dp") // 2
    both = plus(keep, came).astype(jnp.bfloat16)
    return [lax.dynamic_index_in_dim(both, chip ^ k, 0, keepdims=False) for k in range(chip_count())]


def body(enc_in, dec_in, cotangent, w_proj, w_skip, m_proj, v_proj, m_skip, v_skip):
    micro, tokens_here, width = enc_in.shape[1:]
    rows = micro * tokens_here
    enc_rows = enc_in[0].reshape(rows, width)
    dec_rows = dec_in[0].reshape(rows, width)
    out_grad = cotangent[0].reshape(rows, width)
    together = lax.optimization_barrier

    enc_cuts = [rows * n // 8 for n in (5, 7)]
    proj_half, skip_half = w_proj[0].astype(jnp.bfloat16), w_skip[0].astype(jnp.bfloat16)
    stride = skip_half.shape[0]
    cut = stride // 48 * 16
    proj_piece = to_partner(proj_half)
    head = gather_first(skip_half[:cut])
    proj_piece, head, tail, enc0 = together((proj_piece, head, skip_half[cut:], enc_rows[: enc_cuts[0]]))
    enc0 = to_partner(enc0)
    proj_found = gather_first(proj_piece)
    tail = gather_first(tail)
    enc0, proj_found, tail, head, enc1 = together((enc0, proj_found, tail, head, enc_rows[enc_cuts[0] : enc_cuts[1]]))
    enc1 = to_partner(enc1)
    skip_w = [assemble(head), assemble(tail)]
    skip_last = [gather_last(head), gather_last(tail)]
    enc1, proj_found, skip_w, skip_last, enc2 = together(
        (enc1, proj_found, skip_w, skip_last, enc_rows[enc_cuts[1] :])
    )
    enc2 = to_partner(enc2)
    proj_last = gather_last(proj_found)
    proj_whole = assemble(proj_found)
    skip_w = [assemble(last, whole) for last, whole in zip(skip_last, skip_w)]
    skip_parts = [(cut, 0, stride), (stride - cut, cut, stride)]
    (from_dec,) = row_call(decoder_part, [dec_rows], skip_w, skip_parts, 1, 256, 20, out_type=jnp.float32, half=0)
    enc2, proj_last, proj_whole, from_dec, skip_w = together((enc2, proj_last, proj_whole, from_dec, skip_w))
    proj_whole = assemble(proj_last, proj_whole)
    enc_other = (enc0, enc1, enc2)

    skip = project(enc_other, proj_whole, 20)
    dec_out, pre_grad, skip_grad = row_call(
        middle, [from_dec, skip, out_grad], skip_w, skip_parts, 3, 512, 30, half=1
    )
    cuts = [0] + [rows * n // 8 for n in (1, 3, 4, 8)]

    def back(n, value):
        return row_call(
            project_back, [value], [proj_whole], [(1, 0, 1)], 1, 256, 16, start=cuts[n], rows=cuts[n + 1] - cuts[n]
        )[0]

    grad_proj = weight_grad([enc_other], skip_grad)
    grad_proj, skip_grad = together((grad_proj, skip_grad))
    proj_keep, proj_came = pair_send(grad_proj)
    enc0 = back(0, skip_grad)
    enc1 = back(1, skip_grad)
    proj_keep, proj_came, enc0, enc1, pre_grad, skip_grad = together(
        (proj_keep, proj_came, enc0, enc1, pre_grad, skip_grad)
    )
    enc0 = to_partner(enc0)
    proj_blocks = pair_sum(proj_keep, proj_came)
    proj_near = scatter_near(proj_blocks)
    skip_keep, skip_send = pair_split(weight_grad([(dec_rows,), (skip,)], pre_grad))
    enc0, proj_blocks, proj_near, skip_keep, skip_send, enc1, skip_grad = together(
        (enc0, proj_blocks, proj_near, skip_keep, skip_send, enc1, skip_grad)
    )
    enc1 = to_partner(enc1)
    proj_on = scatter_on(proj_blocks, proj_near)
    proj_one = chip_flip(proj_blocks[1], 1)
    skip_came = core_flip(skip_send)
    enc2 = back(2, skip_grad)
    enc3 = back(3, skip_grad)
    enc1, proj_blocks, proj_on, proj_one, skip_keep, skip_came, enc2, enc3 = together(
        (enc1, proj_blocks, proj_on, proj_one, skip_keep, skip_came, enc2, enc3)
    )
    enc2 = to_partner(enc2)
    proj_sum = to_partner(plus(proj_blocks[0], proj_one, *proj_on).astype(jnp.bfloat16))
    skip_blocks = pair_sum(skip_keep, skip_came)
    skip_near = scatter_near(skip_blocks)
    enc2, proj_sum, skip_blocks, skip_near, enc3, pre_grad = together(
        (enc2, proj_sum, skip_blocks, skip_near, enc3, pre_grad)
    )
    proj_sum = proj_sum.astype(jnp.float32)
    enc3 = to_partner(enc3)
    skip_on = scatter_on(skip_blocks, skip_near)
    skip_one = chip_flip(skip_blocks[1], 1)
    skip_sum = plus(skip_blocks[0], skip_one, *skip_on)
    (dec_grad,) = row_call(project_back, [pre_grad], skip_w, skip_parts, 1, 256, 20, half=0)
    enc_grad = jnp.zeros_like(enc_rows)
    for at, part in zip(cuts, (enc0, enc1, enc2, enc3)):
        enc_grad = lax.dynamic_update_slice(enc_grad, part, (at, 0))

    new_proj = adam_update(w_proj[0], m_proj[0], v_proj[0], proj_sum)
    new_skip = adam_update(w_skip[0], m_skip[0], v_skip[0], skip_sum)
    streams = tuple(value.reshape(1, micro, tokens_here, width) for value in (dec_out, enc_grad, dec_grad))
    return streams + tuple(value[None] for value in new_proj + new_skip)


def solution(mesh):
    tokens = P("section", None, "dp", None)
    weights = P("section", "dp", None)
    return jax.shard_map(
        body,
        mesh=mesh,
        in_specs=(tokens,) * 3 + (weights,) * 6,
        out_specs=(tokens,) * 3 + (weights,) * 6,
        check_vma=False,
    )
```

```python
import math

import jax
import jax.numpy as jnp
from jax import lax
from jax.experimental import pallas as pl
from jax.experimental.pallas import tpu as pltpu
from jax.sharding import PartitionSpec as P

half_root = 0.7071067811865476
gauss_norm = 0.3989422804014327
beta_one = 0.9
beta_two = 0.95
learn_rate = 0.002
adam_eps = 1e-08
correct_one = 1.0 - 0.9**10
correct_two = 1.0 - 0.95**10


def gelu_parts(preact):
    normal_cdf = 0.5 * (1.0 + lax.erf(preact * half_root))
    density = jnp.exp(-0.5 * preact * preact) * gauss_norm
    return (preact * normal_cdf, normal_cdf + preact * density)


def adam_update(weight, moment, second, grad):
    new_moment = beta_one * moment + (1.0 - beta_one) * grad
    new_second = beta_two * second + (1.0 - beta_two) * grad * grad
    step_size = new_moment / correct_one / (jnp.sqrt(new_second / correct_two) + adam_eps)
    return (weight - learn_rate * step_size, new_moment, new_second)


def to_partner(value):
    count = lax.axis_size("section")
    pairs = [(s, (s + count // 2) % count) for s in range(count)]
    return lax.ppermute(value, "section", pairs)


def chip_count():
    return lax.axis_size("dp") // 2


def to_chips(value, pairs):
    return lax.ppermute(value, "dp", [(2 * a + c, 2 * b + c) for a, b in pairs for c in range(2)])


def chip_flip(value, mask):
    return to_chips(value, [(z, z ^ mask) for z in range(chip_count())])


def core_flip(value):
    return lax.ppermute(value, "dp", [(d, d ^ 1) for d in range(lax.axis_size("dp"))])


def gather_first(piece):
    found = {0: piece}
    step = chip_count() // 2
    while step > 1:
        found.update({k + step: chip_flip(found[k], step) for k in sorted(found)})
        step //= 2
    found[1] = chip_flip(piece, 1)
    return found


def gather_last(found):
    return {k + 1: chip_flip(found[k], 1) for k in range(2, chip_count(), 2)}


def plus(*terms):
    total = terms[0].astype(jnp.float32)
    for term in terms[1:]:
        total = total + term.astype(jnp.float32)
    return total


def scatter_near(blocks):
    return {k: chip_flip(blocks[k + 1], 1) for k in range(2, len(blocks), 2)}


def scatter_on(blocks, came):
    held = {k: plus(blocks[k], came[k]).astype(jnp.bfloat16) for k in came}
    step = 2
    while step < len(blocks) // 2:
        for k in range(2 * step, len(blocks), 2 * step):
            held[k] = plus(held[k], chip_flip(held[k + step], step)).astype(jnp.bfloat16)
        step *= 2
    return [chip_flip(held[2**n], 2**n) for n in range(1, len(blocks).bit_length() - 1)]


def assemble(found, whole=None):
    place = lax.axis_index("dp")
    chip, core = place // 2, place % 2
    rows, width = found[min(found)].shape
    if whole is None:
        whole = jnp.zeros((2 * chip_count() * rows, width), found[0].dtype)
    whole = whole.reshape(chip_count(), 2, rows, width)
    for k, piece in found.items():
        whole = lax.dynamic_update_slice(whole, piece[None, None], (chip ^ k, core, 0, 0))
        whole = lax.dynamic_update_slice(whole, core_flip(piece)[None, None], (chip ^ k, 1 - core, 0, 0))
    return whole.reshape(-1, width)


def interleave(parts, refs, target, sems, half):
    copies = []
    for (rows, start, stride), ref in zip(parts, refs):
        if rows == stride:
            copies.append(pltpu.make_async_copy(ref, target, sems.at[len(copies)]))
            continue
        count = ref.shape[0] // rows
        taken = range(count) if half is None else range(half * count // 2, (half + 1) * count // 2)
        for d in taken:
            to = (d - taken[0]) * stride + start
            copies.append(
                pltpu.make_async_copy(
                    ref.at[pl.ds(d * rows, rows)], target.at[pl.ds(to, rows)], sems.at[len(copies)]
                )
            )
    for copy in copies:
        copy.start()
    for copy in copies:
        copy.wait()


def copy_count(weights, parts):
    return sum(1 if rows == stride else w.shape[0] // rows for w, (rows, _, stride) in zip(weights, parts))


def row_call(compute, row_arrays, weights, parts, out_count, tile_rows, vmem_mib, start=0, rows=None, out_type=jnp.bfloat16, half=None):
    width = row_arrays[0].shape[1]
    rows = rows or row_arrays[0].shape[0]
    tile = math.gcd(math.gcd(rows, start), tile_rows)
    count = copy_count(weights, parts)

    def kernel(*refs):
        ins = refs[: len(row_arrays)]
        weight_refs = refs[len(row_arrays) : len(row_arrays) + len(weights)]
        outs = refs[len(row_arrays) + len(weights) :][:out_count]
        whole, sems = refs[-2:]

        @pl.when(pl.program_id(0) == 0)
        def _():
            interleave(parts, weight_refs, whole, sems, half)

        compute(ins, whole, outs)

    block = pl.BlockSpec((tile, width), lambda i: (i, 0))
    taken = pl.BlockSpec((tile, width), lambda i: (i + start // tile, 0))
    return pl.pallas_call(
        kernel,
        grid=(rows // tile,),
        in_specs=[taken] * len(row_arrays) + [pl.BlockSpec(memory_space=pl.ANY)] * len(weights),
        out_specs=[block] * out_count,
        out_shape=[jax.ShapeDtypeStruct((rows, width), out_type)] * out_count,
        scratch_shapes=[
            pltpu.VMEM((sum(w.shape[0] for w in weights) // (1 if half is None else 2), width), jnp.bfloat16),
            pltpu.SemaphoreType.DMA((count,)),
        ],
        compiler_params=pltpu.CompilerParams(vmem_limit_bytes=vmem_mib * 2**20),
        cost_estimate=pl.CostEstimate(flops=COST, bytes_accessed=COST, transcendentals=0),
    )(*row_arrays, *weights)


COST = 1000


def dot_nn(left, right):
    return jnp.dot(left, right, preferred_element_type=jnp.float32)


def dot_nt(left, right):
    return lax.dot_general(left, right, (((1,), (1,)), ((), ())), preferred_element_type=jnp.float32)


def dot_tn(left, right):
    return lax.dot_general(left, right, (((0,), (0,)), ((), ())), preferred_element_type=jnp.float32)


def project(parts, weight, vmem_mib):
    width = weight.shape[1]
    rows = sum(part.shape[0] for part in parts)

    def kernel(*refs):
        at = 0
        for ref, part in zip(refs, parts):
            refs[-1][at : at + part.shape[0]] = dot_nn(ref[...], refs[-2][...]).astype(jnp.bfloat16)
            at += part.shape[0]

    return pl.pallas_call(
        kernel,
        out_shape=jax.ShapeDtypeStruct((rows, width), jnp.bfloat16),
        compiler_params=pltpu.CompilerParams(vmem_limit_bytes=vmem_mib * 2**20),
        cost_estimate=pl.CostEstimate(flops=COST, bytes_accessed=COST, transcendentals=0),
    )(*parts, weight)


def project_back(ins, whole, outs):
    outs[0][...] = dot_nt(ins[0][...], whole[...]).astype(jnp.bfloat16)


def decoder_part(ins, whole, outs):
    outs[0][...] = dot_nn(ins[0][...], whole[...])


def middle(ins, whole, outs):
    from_dec, skip, out_grad = ins
    rows, width = skip.shape
    part = math.gcd(rows, 256)
    for at in range(0, rows, part):
        here = slice(at, at + part)
        preact = from_dec[here] + dot_nn(skip[here], whole[...])
        activated, gelu_slope = gelu_parts(preact)
        outs[0][here] = activated.astype(jnp.bfloat16)
        pre_grad = (out_grad[here].astype(jnp.float32) * gelu_slope).astype(jnp.bfloat16)
        outs[1][here] = pre_grad
        outs[2][here] = dot_nt(pre_grad, whole[...]).astype(jnp.bfloat16)


def weight_grad(lefts, right):
    rows, width = right.shape
    tile = math.gcd(width, 384)
    steps = width // tile
    parts = [(n, part) for n, left in enumerate(lefts) for part in left]

    def kernel(*refs):
        step = pl.program_id(0)
        right_ref, out_ref = refs[-2:]
        for n in range(len(lefts)):

            @pl.when(step // steps == n)
            def _(n=n):
                total, at = 0.0, 0
                for ref, (owner, part) in zip(refs, parts):
                    if owner == n:
                        total = total + dot_tn(ref[...], right_ref[at : at + part.shape[0]])
                        at += part.shape[0]
                out_ref[...] = total.astype(jnp.bfloat16)

    def spec(n, part):
        return pl.BlockSpec((part.shape[0], tile), lambda i: (0, jnp.clip(i - n * steps, 0, steps - 1)))

    return pl.pallas_call(
        kernel,
        grid=(len(lefts) * steps,),
        in_specs=[spec(n, part) for n, part in parts]
        + [pl.BlockSpec((rows, width), lambda i: (0, 0), pipeline_mode=pl.Buffered(1))],
        out_specs=pl.BlockSpec((tile, width), lambda i: (i, 0)),
        out_shape=jax.ShapeDtypeStruct((len(lefts) * width, width), jnp.bfloat16),
        compiler_params=pltpu.CompilerParams(vmem_limit_bytes=16 * 2**20),
        cost_estimate=pl.CostEstimate(flops=COST, bytes_accessed=COST, transcendentals=0),
    )(*[part for _, part in parts], right)


def pair_split(total):
    core = lax.axis_index("dp") % 2
    split = total.reshape(chip_count(), 2, -1, total.shape[1])
    keep = lax.dynamic_index_in_dim(split, core, 1, keepdims=False)
    return keep, lax.dynamic_index_in_dim(split, 1 - core, 1, keepdims=False)


def pair_send(total):
    keep, send = pair_split(total)
    return keep, core_flip(send)


def pair_sum(keep, came):
    chip = lax.axis_index("dp") // 2
    both = plus(keep, came).astype(jnp.bfloat16)
    return [lax.dynamic_index_in_dim(both, chip ^ k, 0, keepdims=False) for k in range(chip_count())]


def body(enc_in, dec_in, cotangent, w_proj, w_skip, m_proj, v_proj, m_skip, v_skip):
    micro, tokens_here, width = enc_in.shape[1:]
    rows = micro * tokens_here
    enc_rows = enc_in[0].reshape(rows, width)
    dec_rows = dec_in[0].reshape(rows, width)
    out_grad = cotangent[0].reshape(rows, width)
    together = lax.optimization_barrier

    enc_cuts = [rows * n // 8 for n in (5, 7)]
    proj_half, skip_half = w_proj[0].astype(jnp.bfloat16), w_skip[0].astype(jnp.bfloat16)
    stride = skip_half.shape[0]
    cut = stride // 48 * 16
    proj_piece = to_partner(proj_half)
    head = gather_first(skip_half[:cut])
    proj_piece, head, tail, enc0 = together((proj_piece, head, skip_half[cut:], enc_rows[: enc_cuts[0]]))
    enc0 = to_partner(enc0)
    proj_found = gather_first(proj_piece)
    tail = gather_first(tail)
    enc0, proj_found, tail, head, enc1 = together((enc0, proj_found, tail, head, enc_rows[enc_cuts[0] : enc_cuts[1]]))
    enc1 = to_partner(enc1)
    skip_w = [assemble(head), assemble(tail)]
    skip_last = [gather_last(head), gather_last(tail)]
    enc1, proj_found, skip_w, skip_last, enc2 = together(
        (enc1, proj_found, skip_w, skip_last, enc_rows[enc_cuts[1] :])
    )
    enc2 = to_partner(enc2)
    proj_last = gather_last(proj_found)
    proj_whole = assemble(proj_found)
    skip_w = [assemble(last, whole) for last, whole in zip(skip_last, skip_w)]
    skip_parts = [(cut, 0, stride), (stride - cut, cut, stride)]
    (from_dec,) = row_call(decoder_part, [dec_rows], skip_w, skip_parts, 1, 256, 20, out_type=jnp.float32, half=0)
    enc2, proj_last, proj_whole, from_dec, skip_w = together((enc2, proj_last, proj_whole, from_dec, skip_w))
    proj_whole = assemble(proj_last, proj_whole)
    enc_other = (enc0, enc1, enc2)

    skip = project(enc_other, proj_whole, 20)
    dec_out, pre_grad, skip_grad = row_call(
        middle, [from_dec, skip, out_grad], skip_w, skip_parts, 3, 512, 30, half=1
    )
    cuts = [0] + [rows * n // 8 for n in (1, 3, 4, 8)]

    def back(n, value):
        return row_call(
            project_back, [value], [proj_whole], [(1, 0, 1)], 1, 256, 16, start=cuts[n], rows=cuts[n + 1] - cuts[n]
        )[0]

    grad_proj = weight_grad([enc_other], skip_grad)
    grad_proj, skip_grad = together((grad_proj, skip_grad))
    proj_keep, proj_came = pair_send(grad_proj)
    enc0 = back(0, skip_grad)
    enc1 = back(1, skip_grad)
    proj_keep, proj_came, enc0, enc1, pre_grad, skip_grad = together(
        (proj_keep, proj_came, enc0, enc1, pre_grad, skip_grad)
    )
    enc0 = to_partner(enc0)
    proj_blocks = pair_sum(proj_keep, proj_came)
    proj_near = scatter_near(proj_blocks)
    skip_keep, skip_send = pair_split(weight_grad([(dec_rows,), (skip,)], pre_grad))
    enc0, proj_blocks, proj_near, skip_keep, skip_send, enc1, skip_grad = together(
        (enc0, proj_blocks, proj_near, skip_keep, skip_send, enc1, skip_grad)
    )
    enc1 = to_partner(enc1)
    proj_on = scatter_on(proj_blocks, proj_near)
    proj_one = chip_flip(proj_blocks[1], 1)
    skip_came = core_flip(skip_send)
    enc2 = back(2, skip_grad)
    enc3 = back(3, skip_grad)
    enc1, proj_blocks, proj_on, proj_one, skip_keep, skip_came, enc2, enc3 = together(
        (enc1, proj_blocks, proj_on, proj_one, skip_keep, skip_came, enc2, enc3)
    )
    enc2 = to_partner(enc2)
    proj_sum = to_partner(plus(proj_blocks[0], proj_one, *proj_on).astype(jnp.bfloat16))
    skip_blocks = pair_sum(skip_keep, skip_came)
    skip_near = scatter_near(skip_blocks)
    enc2, proj_sum, skip_blocks, skip_near, enc3, pre_grad = together(
        (enc2, proj_sum, skip_blocks, skip_near, enc3, pre_grad)
    )
    proj_sum = proj_sum.astype(jnp.float32)
    enc3 = to_partner(enc3)
    skip_on = scatter_on(skip_blocks, skip_near)
    skip_one = chip_flip(skip_blocks[1], 1)
    (dec_grad,) = row_call(project_back, [pre_grad], skip_w, skip_parts, 1, 256, 20, half=0)
    enc_grad = jnp.zeros_like(enc_rows)
    for at, part in zip(cuts, (enc0, enc1, enc2, enc3)):
        enc_grad = lax.dynamic_update_slice(enc_grad, part, (at, 0))
    enc_grad, skip_one = together((enc_grad, skip_one))
    skip_sum = plus(skip_blocks[0], skip_one, *skip_on)

    new_proj = adam_update(w_proj[0], m_proj[0], v_proj[0], proj_sum)
    new_skip = adam_update(w_skip[0], m_skip[0], v_skip[0], skip_sum)
    streams = tuple(value.reshape(1, micro, tokens_here, width) for value in (dec_out, enc_grad, dec_grad))
    return streams + tuple(value[None] for value in new_proj + new_skip)


def solution(mesh):
    tokens = P("section", None, "dp", None)
    weights = P("section", "dp", None)
    return jax.shard_map(
        body,
        mesh=mesh,
        in_specs=(tokens,) * 3 + (weights,) * 6,
        out_specs=(tokens,) * 3 + (weights,) * 6,
        check_vma=False,
    )
```

```python
import math

import jax
import jax.numpy as jnp
from jax import lax
from jax.experimental import pallas as pl
from jax.experimental.pallas import tpu as pltpu
from jax.sharding import PartitionSpec as P

half_root = 0.7071067811865476
gauss_norm = 0.3989422804014327
beta_one = 0.9
beta_two = 0.95
learn_rate = 0.002
adam_eps = 1e-08
correct_one = 1.0 - 0.9**10
correct_two = 1.0 - 0.95**10


def gelu_parts(preact):
    normal_cdf = 0.5 * (1.0 + lax.erf(preact * half_root))
    density = jnp.exp(-0.5 * preact * preact) * gauss_norm
    return (preact * normal_cdf, normal_cdf + preact * density)


def adam_update(weight, moment, second, grad):
    new_moment = beta_one * moment + (1.0 - beta_one) * grad
    new_second = beta_two * second + (1.0 - beta_two) * grad * grad
    step_size = new_moment / correct_one / (jnp.sqrt(new_second / correct_two) + adam_eps)
    return (weight - learn_rate * step_size, new_moment, new_second)


def to_partner(value):
    count = lax.axis_size("section")
    pairs = [(s, (s + count // 2) % count) for s in range(count)]
    return lax.ppermute(value, "section", pairs)


def chip_count():
    return lax.axis_size("dp") // 2


def to_chips(value, pairs):
    return lax.ppermute(value, "dp", [(2 * a + c, 2 * b + c) for a, b in pairs for c in range(2)])


def chip_flip(value, mask):
    return to_chips(value, [(z, z ^ mask) for z in range(chip_count())])


def core_flip(value):
    return lax.ppermute(value, "dp", [(d, d ^ 1) for d in range(lax.axis_size("dp"))])


def gather_first(piece):
    found = {0: piece}
    step = chip_count() // 2
    while step > 1:
        found.update({k + step: chip_flip(found[k], step) for k in sorted(found)})
        step //= 2
    found[1] = chip_flip(piece, 1)
    return found


def gather_last(found):
    return {k + 1: chip_flip(found[k], 1) for k in range(2, chip_count(), 2)}


def plus(*terms):
    total = terms[0].astype(jnp.float32)
    for term in terms[1:]:
        total = total + term.astype(jnp.float32)
    return total


def scatter_near(blocks):
    return {k: chip_flip(blocks[k + 1], 1) for k in range(2, len(blocks), 2)}


def scatter_on(blocks, came):
    held = {k: plus(blocks[k], came[k]).astype(jnp.bfloat16) for k in came}
    step = 2
    while step < len(blocks) // 2:
        for k in range(2 * step, len(blocks), 2 * step):
            held[k] = plus(held[k], chip_flip(held[k + step], step)).astype(jnp.bfloat16)
        step *= 2
    return [chip_flip(held[2**n], 2**n) for n in range(1, len(blocks).bit_length() - 1)]


def assemble(found, whole=None):
    place = lax.axis_index("dp")
    chip, core = place // 2, place % 2
    rows, width = found[min(found)].shape
    if whole is None:
        whole = jnp.zeros((2 * chip_count() * rows, width), found[0].dtype)
    whole = whole.reshape(chip_count(), 2, rows, width)
    for k, piece in found.items():
        whole = lax.dynamic_update_slice(whole, piece[None, None], (chip ^ k, core, 0, 0))
        whole = lax.dynamic_update_slice(whole, core_flip(piece)[None, None], (chip ^ k, 1 - core, 0, 0))
    return whole.reshape(-1, width)


def interleave(parts, refs, target, sems, half):
    copies = []
    for (rows, start, stride), ref in zip(parts, refs):
        if rows == stride:
            copies.append(pltpu.make_async_copy(ref, target, sems.at[len(copies)]))
            continue
        count = ref.shape[0] // rows
        taken = range(count) if half is None else range(half * count // 2, (half + 1) * count // 2)
        for d in taken:
            to = (d - taken[0]) * stride + start
            copies.append(
                pltpu.make_async_copy(
                    ref.at[pl.ds(d * rows, rows)], target.at[pl.ds(to, rows)], sems.at[len(copies)]
                )
            )
    for copy in copies:
        copy.start()
    for copy in copies:
        copy.wait()


def copy_count(weights, parts):
    return sum(1 if rows == stride else w.shape[0] // rows for w, (rows, _, stride) in zip(weights, parts))


def row_call(compute, row_arrays, weights, parts, out_count, tile_rows, vmem_mib, start=0, rows=None, out_type=jnp.bfloat16, half=None):
    width = row_arrays[0].shape[1]
    rows = rows or row_arrays[0].shape[0]
    tile = math.gcd(math.gcd(rows, start), tile_rows)
    count = copy_count(weights, parts)

    def kernel(*refs):
        ins = refs[: len(row_arrays)]
        weight_refs = refs[len(row_arrays) : len(row_arrays) + len(weights)]
        outs = refs[len(row_arrays) + len(weights) :][:out_count]
        whole, sems = refs[-2:]

        @pl.when(pl.program_id(0) == 0)
        def _():
            interleave(parts, weight_refs, whole, sems, half)

        compute(ins, whole, outs)

    block = pl.BlockSpec((tile, width), lambda i: (i, 0))
    taken = pl.BlockSpec((tile, width), lambda i: (i + start // tile, 0))
    return pl.pallas_call(
        kernel,
        grid=(rows // tile,),
        in_specs=[taken] * len(row_arrays) + [pl.BlockSpec(memory_space=pl.ANY)] * len(weights),
        out_specs=[block] * out_count,
        out_shape=[jax.ShapeDtypeStruct((rows, width), out_type)] * out_count,
        scratch_shapes=[
            pltpu.VMEM((sum(w.shape[0] for w in weights) // (1 if half is None else 2), width), jnp.bfloat16),
            pltpu.SemaphoreType.DMA((count,)),
        ],
        compiler_params=pltpu.CompilerParams(vmem_limit_bytes=vmem_mib * 2**20),
        cost_estimate=pl.CostEstimate(flops=COST, bytes_accessed=COST, transcendentals=0),
    )(*row_arrays, *weights)


COST = 1000


def dot_nn(left, right):
    return jnp.dot(left, right, preferred_element_type=jnp.float32)


def dot_nt(left, right):
    return lax.dot_general(left, right, (((1,), (1,)), ((), ())), preferred_element_type=jnp.float32)


def dot_tn(left, right):
    return lax.dot_general(left, right, (((0,), (0,)), ((), ())), preferred_element_type=jnp.float32)


def project(parts, weight, vmem_mib):
    width = weight.shape[1]
    rows = sum(part.shape[0] for part in parts)

    def kernel(*refs):
        at = 0
        for ref, part in zip(refs, parts):
            refs[-1][at : at + part.shape[0]] = dot_nn(ref[...], refs[-2][...]).astype(jnp.bfloat16)
            at += part.shape[0]

    return pl.pallas_call(
        kernel,
        out_shape=jax.ShapeDtypeStruct((rows, width), jnp.bfloat16),
        compiler_params=pltpu.CompilerParams(vmem_limit_bytes=vmem_mib * 2**20),
        cost_estimate=pl.CostEstimate(flops=COST, bytes_accessed=COST, transcendentals=0),
    )(*parts, weight)


def project_back(ins, whole, outs):
    outs[0][...] = dot_nt(ins[0][...], whole[...]).astype(jnp.bfloat16)


def decoder_part(ins, whole, outs):
    outs[0][...] = dot_nn(ins[0][...], whole[...])


def middle(ins, whole, outs):
    from_dec, skip, out_grad = ins
    rows, width = skip.shape
    part = math.gcd(rows, 256)
    for at in range(0, rows, part):
        here = slice(at, at + part)
        preact = from_dec[here] + dot_nn(skip[here], whole[...])
        activated, gelu_slope = gelu_parts(preact)
        outs[0][here] = activated.astype(jnp.bfloat16)
        pre_grad = (out_grad[here].astype(jnp.float32) * gelu_slope).astype(jnp.bfloat16)
        outs[1][here] = pre_grad
        outs[2][here] = dot_nt(pre_grad, whole[...]).astype(jnp.bfloat16)


def weight_grad(lefts, right):
    rows, width = right.shape
    tile = math.gcd(width, 384)
    steps = width // tile
    parts = [(n, part) for n, left in enumerate(lefts) for part in left]

    def kernel(*refs):
        step = pl.program_id(0)
        right_ref, out_ref = refs[-2:]
        for n in range(len(lefts)):

            @pl.when(step // steps == n)
            def _(n=n):
                total, at = 0.0, 0
                for ref, (owner, part) in zip(refs, parts):
                    if owner == n:
                        total = total + dot_tn(ref[...], right_ref[at : at + part.shape[0]])
                        at += part.shape[0]
                out_ref[...] = total.astype(jnp.bfloat16)

    def spec(n, part):
        return pl.BlockSpec((part.shape[0], tile), lambda i: (0, jnp.clip(i - n * steps, 0, steps - 1)))

    return pl.pallas_call(
        kernel,
        grid=(len(lefts) * steps,),
        in_specs=[spec(n, part) for n, part in parts]
        + [pl.BlockSpec((rows, width), lambda i: (0, 0), pipeline_mode=pl.Buffered(1))],
        out_specs=pl.BlockSpec((tile, width), lambda i: (i, 0)),
        out_shape=jax.ShapeDtypeStruct((len(lefts) * width, width), jnp.bfloat16),
        compiler_params=pltpu.CompilerParams(vmem_limit_bytes=16 * 2**20),
        cost_estimate=pl.CostEstimate(flops=COST, bytes_accessed=COST, transcendentals=0),
    )(*[part for _, part in parts], right)


def pair_split(total):
    core = lax.axis_index("dp") % 2
    split = total.reshape(chip_count(), 2, -1, total.shape[1])
    keep = lax.dynamic_index_in_dim(split, core, 1, keepdims=False)
    return keep, lax.dynamic_index_in_dim(split, 1 - core, 1, keepdims=False)


def pair_send(total):
    keep, send = pair_split(total)
    return keep, core_flip(send)


def pair_sum(keep, came):
    chip = lax.axis_index("dp") // 2
    both = plus(keep, came).astype(jnp.bfloat16)
    return [lax.dynamic_index_in_dim(both, chip ^ k, 0, keepdims=False) for k in range(chip_count())]


def body(enc_in, dec_in, cotangent, w_proj, w_skip, m_proj, v_proj, m_skip, v_skip):
    micro, tokens_here, width = enc_in.shape[1:]
    rows = micro * tokens_here
    enc_rows = enc_in[0].reshape(rows, width)
    dec_rows = dec_in[0].reshape(rows, width)
    out_grad = cotangent[0].reshape(rows, width)
    together = lax.optimization_barrier

    enc_cuts = [rows * n // 8 for n in (5, 7)]
    proj_half, skip_half = w_proj[0].astype(jnp.bfloat16), w_skip[0].astype(jnp.bfloat16)
    stride = skip_half.shape[0]
    cut = stride // 48 * 16
    proj_piece = to_partner(proj_half)
    head = gather_first(skip_half[:cut])
    proj_piece, head, tail, enc0 = together((proj_piece, head, skip_half[cut:], enc_rows[: enc_cuts[0]]))
    enc0 = to_partner(enc0)
    proj_found = gather_first(proj_piece)
    tail = gather_first(tail)
    enc0, proj_found, tail, head, enc1 = together((enc0, proj_found, tail, head, enc_rows[enc_cuts[0] : enc_cuts[1]]))
    enc1 = to_partner(enc1)
    skip_w = [assemble(head), assemble(tail)]
    skip_last = [gather_last(head), gather_last(tail)]
    enc1, proj_found, skip_w, skip_last, enc2 = together(
        (enc1, proj_found, skip_w, skip_last, enc_rows[enc_cuts[1] :])
    )
    enc2 = to_partner(enc2)
    proj_last = gather_last(proj_found)
    proj_whole = assemble(proj_found)
    skip_w = [assemble(last, whole) for last, whole in zip(skip_last, skip_w)]
    skip_parts = [(cut, 0, stride), (stride - cut, cut, stride)]
    (from_dec,) = row_call(decoder_part, [dec_rows], skip_w, skip_parts, 1, 512, 20, out_type=jnp.float32, half=0)
    enc2, proj_last, proj_whole, from_dec, skip_w = together((enc2, proj_last, proj_whole, from_dec, skip_w))
    proj_whole = assemble(proj_last, proj_whole)
    enc_other = (enc0, enc1, enc2)

    skip = project(enc_other, proj_whole, 20)
    dec_out, pre_grad, skip_grad = row_call(
        middle, [from_dec, skip, out_grad], skip_w, skip_parts, 3, 512, 30, half=1
    )
    cuts = [0] + [rows * n // 8 for n in (1, 3, 4, 8)]

    def back(n, value):
        return row_call(
            project_back, [value], [proj_whole], [(1, 0, 1)], 1, 256, 16, start=cuts[n], rows=cuts[n + 1] - cuts[n]
        )[0]

    grad_proj = weight_grad([enc_other], skip_grad)
    grad_proj, skip_grad = together((grad_proj, skip_grad))
    proj_keep, proj_came = pair_send(grad_proj)
    enc0 = back(0, skip_grad)
    enc1 = back(1, skip_grad)
    proj_keep, proj_came, enc0, enc1, pre_grad, skip_grad = together(
        (proj_keep, proj_came, enc0, enc1, pre_grad, skip_grad)
    )
    enc0 = to_partner(enc0)
    proj_blocks = pair_sum(proj_keep, proj_came)
    proj_near = scatter_near(proj_blocks)
    skip_keep, skip_send = pair_split(weight_grad([(dec_rows,), (skip,)], pre_grad))
    enc0, proj_blocks, proj_near, skip_keep, skip_send, enc1, skip_grad = together(
        (enc0, proj_blocks, proj_near, skip_keep, skip_send, enc1, skip_grad)
    )
    enc1 = to_partner(enc1)
    proj_on = scatter_on(proj_blocks, proj_near)
    proj_one = chip_flip(proj_blocks[1], 1)
    skip_came = core_flip(skip_send)
    enc2 = back(2, skip_grad)
    enc3 = back(3, skip_grad)
    enc1, proj_blocks, proj_on, proj_one, skip_keep, skip_came, enc2, enc3 = together(
        (enc1, proj_blocks, proj_on, proj_one, skip_keep, skip_came, enc2, enc3)
    )
    enc2 = to_partner(enc2)
    proj_sum = to_partner(plus(proj_blocks[0], proj_one, *proj_on).astype(jnp.bfloat16))
    skip_blocks = pair_sum(skip_keep, skip_came)
    skip_near = scatter_near(skip_blocks)
    enc2, proj_sum, skip_blocks, skip_near, enc3, pre_grad = together(
        (enc2, proj_sum, skip_blocks, skip_near, enc3, pre_grad)
    )
    proj_sum = proj_sum.astype(jnp.float32)
    enc3 = to_partner(enc3)
    skip_on = scatter_on(skip_blocks, skip_near)
    skip_one = chip_flip(skip_blocks[1], 1)
    (dec_grad,) = row_call(project_back, [pre_grad], skip_w, skip_parts, 1, 256, 20, half=0)
    enc_grad = jnp.zeros_like(enc_rows)
    for at, part in zip(cuts, (enc0, enc1, enc2, enc3)):
        enc_grad = lax.dynamic_update_slice(enc_grad, part, (at, 0))
    enc_grad, skip_one = together((enc_grad, skip_one))
    skip_sum = plus(skip_blocks[0], skip_one, *skip_on)

    new_proj = adam_update(w_proj[0], m_proj[0], v_proj[0], proj_sum)
    new_skip = adam_update(w_skip[0], m_skip[0], v_skip[0], skip_sum)
    streams = tuple(value.reshape(1, micro, tokens_here, width) for value in (dec_out, enc_grad, dec_grad))
    return streams + tuple(value[None] for value in new_proj + new_skip)


def solution(mesh):
    tokens = P("section", None, "dp", None)
    weights = P("section", "dp", None)
    return jax.shard_map(
        body,
        mesh=mesh,
        in_specs=(tokens,) * 3 + (weights,) * 6,
        out_specs=(tokens,) * 3 + (weights,) * 6,
        check_vma=False,
    )
```
